32 devices in a mesh: dp: 16 (over z, x, core), expert: 2 (over y).
Axes of the slice: x: 2, y: 2, z: 4, core: 2. Of those that a mesh axis runs over, the one named last changes fastest.
Arguments:
- tokens: bfloat16 [4096, 2048], P(('dp', 'expert')), may hold values from -6 to 6
- expert_ids: int32 [4096, 8], P(('dp', 'expert')), may hold values from 0 to 16, as said below
- gate_weights: float32 [4096, 8], P(('dp', 'expert')), may hold values from 0.2 to 1
- hot_weights: bfloat16 [1, 3, 768, 2048], P(None, None, 'expert'), may hold values from -0.125 to 0.125
- cold_weights: bfloat16 [16, 3, 768, 2048], P('dp'), may hold values from -0.125 to 0.125
Outputs:
- combined: bfloat16 [4096, 2048], P(('dp', 'expert'))
The draws below stay inside these ranges and needn't reach their ends.
Inputs may be any that keep to these rules, and one draw needn't show every extreme that they name: `expert_ids`: each row names 8 different experts; among the rows of one device expert 0 is named by exactly 80 rows and no other expert by more than 80 rows.
All inputs are finite; a program needn't handle non-finite values.
Results may differ from the reference program's by a relative error of at most 0.0057.
Values may be sent and summed in bfloat16 or wider, within the bound.
No kernel may reach another device: no remote copies, remote signals or barrier semaphores. Data moves between devices by JAX's collectives and lax.ppermute only.
A program may use at most 128 MiB of HBM per device.

```python
import jax
import jax.numpy as jnp
from jax import lax

D = 2048
FF = 768
TOP = 8
HOT = 1
COLD_DEV = 1
TOK_DEV = 128
EXPERTS = 17
CAP = 80
TOKENS = 4096
N_DP = 16


def draw_expert_ids(key, part):
    key = jax.random.fold_in(key, 11)
    blocks = TOKENS // TOK_DEV
    cold_count = EXPERTS - 1

    def one_block(index):
        block_key = jax.random.fold_in(key, index)
        key_rows, key_labels, key_start, key_roll = jax.random.split(block_key, 4)
        row_order = jax.random.permutation(key_rows, TOK_DEV).astype(jnp.int32)
        placed = jnp.zeros((TOK_DEV,), jnp.int32).at[row_order].set(jnp.arange(TOK_DEV, dtype=jnp.int32))
        has_hot = (placed < CAP).astype(jnp.int32)
        needed = TOP - has_hot
        offset = jax.random.randint(key_start, (), 0, cold_count).astype(jnp.int32)
        starts = jnp.cumsum(needed) - needed + offset
        column = jnp.arange(TOP, dtype=jnp.int32)[None, :]
        position = (starts[:, None] + column - has_hot[:, None]) % cold_count
        labels = jax.random.permutation(key_labels, cold_count).astype(jnp.int32)
        values = jnp.where((has_hot[:, None] == 1) & (column == 0), 0, 1 + labels[position])
        shifts = jax.random.randint(key_roll, (TOK_DEV, 1), 0, TOP).astype(jnp.int32)
        return jnp.take_along_axis(values, (column + shifts) % TOP, axis=1)
    drawn = lax.map(one_block, jnp.arange(blocks, dtype=jnp.int32))
    return drawn.reshape(TOKENS, TOP).astype(jnp.int32)


def level_of(stream_key, dims, shards, low, high):
    gain, own = 1.0, jax.random.fold_in(stream_key, 6)
    for dim, parts in shards:
        draws = jnp.exp(jax.random.uniform(jax.random.fold_in(own, dim), (parts,), jnp.float32, low / len(shards), high / len(shards)))
        gain = gain * jnp.repeat(draws, dims[dim] // parts).reshape([-1 if axis == dim else 1 for axis in range(len(dims))])
    return gain


def bell_draw(stream_key, extent, deviation, reach, shards=(), held_as=jnp.bfloat16):
    entries = deviation * jax.random.normal(stream_key, extent, jnp.float32)
    if shards:
        entries = entries * level_of(stream_key, extent, shards, -0.22, 0.18)
    return jnp.clip(entries, -reach, reach).astype(held_as)


def setup_inputs(seed: int = 0) -> dict:
    streams_of = jax.random.split(jax.random.key(seed), 6)
    return {
        "tokens": bell_draw(streams_of[0], (TOKENS, D), 1.0, 6.0, ((0, 32),)),
        "expert_ids": draw_expert_ids(jax.random.fold_in(streams_of[5], 71), 0),
        "gate_weights": jnp.clip(0.2 + 0.8 * jax.random.uniform(streams_of[2], (TOKENS, TOP), jnp.float32) ** level_of(streams_of[2], (TOKENS, TOP), ((0, 32),), -0.2, 0.2), 0.2, 1.0),
        "hot_weights": bell_draw(streams_of[3], (HOT, 3, FF, D), D ** -0.5, 0.125, ((2, 2),)),
        "cold_weights": bell_draw(streams_of[4], (COLD_DEV * N_DP, 3, FF, D), D ** -0.5, 0.125, ((0, 16),)),
    }


def expert_apply(inputs, weights):
    gate_part = jnp.dot(inputs, weights[0].T, preferred_element_type=jnp.float32)
    up_part = jnp.dot(inputs, weights[1].T, preferred_element_type=jnp.float32)
    hidden = (jax.nn.silu(gate_part) * up_part).astype(jnp.bfloat16)
    return jnp.dot(hidden, weights[2], preferred_element_type=jnp.float32).astype(jnp.bfloat16)


def reference(tokens, expert_ids, gate_weights, hot_weights, cold_weights):
    tables = jnp.concatenate([hot_weights, cold_weights], axis=0)
    flat_ids = expert_ids.reshape(-1).astype(jnp.int32)
    ordering = jnp.argsort(flat_ids, stable=True).astype(jnp.int32)
    sorted_ids = flat_ids[ordering]
    labels = jnp.arange(EXPERTS, dtype=jnp.int32)
    begins = jnp.searchsorted(sorted_ids, labels, side="left").astype(jnp.int32)
    finish = jnp.searchsorted(sorted_ids, labels, side="right").astype(jnp.int32)
    longest = CAP * (TOKENS // TOK_DEV)
    padded_order = jnp.concatenate([ordering, jnp.zeros((longest,), jnp.int32)])
    gate_flat = gate_weights.reshape(-1)

    def add_expert(expert, summed):
        chosen = lax.dynamic_slice(padded_order, (begins[expert].astype(jnp.int32),), (longest,))
        active = jnp.arange(longest, dtype=jnp.int32) < (finish[expert] - begins[expert])
        owners = chosen // TOP
        gathered = tokens[owners]
        output = expert_apply(gathered, tables[expert])
        factor = jnp.where(active, gate_flat[chosen], jnp.zeros((), gate_flat.dtype))
        return summed.at[owners].add(output.astype(summed.dtype) * factor[:, None])

    summed = lax.fori_loop(0, EXPERTS, add_expert, jnp.zeros((TOKENS, D), jnp.float32))
    return summed.astype(jnp.bfloat16)
```

```python
import functools

import jax
import jax.numpy as jnp
from jax import lax
from jax.experimental import pallas as pl
from jax.experimental.pallas import tpu as pltpu
from jax.sharding import PartitionSpec as P

LANES = 128
NT = (((1,), (1,)), ((), ()))


def shifted(block, axis, by):
    size = lax.axis_size(axis)
    return lax.ppermute(block, axis, [(i, (i + by) % size) for i in range(size)])


def ring_pairs(count):
    chips = count // 2
    half = chips // 2

    def first_core(place):
        place %= chips
        return 4 * place if place < half else 4 * (chips - 1 - place) + 2

    onward = [
        (first_core(place) + core, first_core(place + 1) + core)
        for place in range(chips)
        for core in range(2)
    ]
    return onward, [(target, source) for source, target in onward]


def expert_kernel(parts, kept_rows, features, scaled, owner_ref, *refs):
    blocks, (gate_ref, up_ref, down_ref, keep_ref, send_ref, inputs, scale, total) = (
        refs[:parts],
        refs[parts:],
    )
    step = pl.program_id(0)

    @pl.when(step == 0)
    def _():
        row = 0
        for block in blocks:
            rows = block.shape[0]
            inputs[row : row + rows, :] = block[:, :features]
            if scaled:
                extra = block[:, features:].astype(jnp.float32)
                lane = lax.broadcasted_iota(jnp.int32, extra.shape, 1)
                owner, count = owner_ref[0], owner_ref[1]
                mine = (lane == owner) | (lane == owner + count) | (lane == owner + 2 * count)
                scale[row : row + rows, :] = jnp.sum(
                    jnp.where(mine, extra, 0.0), axis=1, keepdims=True
                )
            row += rows

    values = inputs[...]
    gate = lax.dot_general(values, gate_ref[0, 0], NT, preferred_element_type=jnp.float32)
    up = lax.dot_general(values, up_ref[0, 0], NT, preferred_element_type=jnp.float32)
    hidden = (gate / (1.0 + jnp.exp(-gate)) * up).astype(jnp.bfloat16)
    partial = jnp.dot(hidden, down_ref[0, 0], preferred_element_type=jnp.float32)

    @pl.when(step == 0)
    def _():
        total[...] = partial

    @pl.when(step > 0)
    def _():
        total[...] += partial

    @pl.when(step == pl.num_programs(0) - 1)
    def _():
        result = total[...]
        if scaled:
            result = result * scale[...]
        keep_ref[...] = result[:kept_rows]
        send_ref[...] = result[kept_rows:].astype(jnp.bfloat16)


def expert_apply(blocks, weights, kept_rows, features, owner, tile):
    scaled = owner is not None
    if owner is None:
        owner = jnp.zeros((2,), jnp.int32)
    rows = sum(block.shape[0] for block in blocks)
    hidden = weights.shape[2]
    tile = min(tile, hidden)
    whole = [pl.BlockSpec(block.shape, lambda i, owner: (0, 0)) for block in blocks]

    def matrix(which):
        return pl.BlockSpec((1, 1, tile, features), lambda i, owner: (0, which, i, 0))

    return pl.pallas_call(
        functools.partial(expert_kernel, len(blocks), kept_rows, features, scaled),
        grid_spec=pltpu.PrefetchScalarGridSpec(
            num_scalar_prefetch=1,
            grid=(hidden // tile,),
            in_specs=whole + [matrix(0), matrix(1), matrix(2)],
            out_specs=[
                pl.BlockSpec((kept_rows, features), lambda i, owner: (0, 0)),
                pl.BlockSpec((rows - kept_rows, features), lambda i, owner: (0, 0)),
            ],
            scratch_shapes=[
                pltpu.VMEM((rows, features), jnp.bfloat16),
                pltpu.VMEM((rows, 1), jnp.float32),
                pltpu.VMEM((rows, features), jnp.float32),
            ],
        ),
        out_shape=[
            jax.ShapeDtypeStruct((kept_rows, features), jnp.float32),
            jax.ShapeDtypeStruct((rows - kept_rows, features), jnp.bfloat16),
        ],
        compiler_params=pltpu.CompilerParams(
            dimension_semantics=("arbitrary",), vmem_limit_bytes=40 * 1024 * 1024
        ),
        cost_estimate=pl.CostEstimate(
            flops=6 * rows * hidden * features,
            bytes_accessed=2 * 3 * hidden * features + 8 * rows * features,
            transcendentals=rows * hidden,
        ),
    )(owner, *blocks, weights, weights, weights)


def on_device(tokens, expert_ids, gate_weights, hot_weights, cold_weights):
    rows, features = tokens.shape
    count = lax.axis_size("dp")
    groups = lax.axis_size("expert")
    experts = 1 + count
    onward, backward = ring_pairs(count)
    across = [(i, i ^ 1) for i in range(count)]
    reach = count // 4
    owner = jnp.stack([lax.axis_index("dp"), count]).astype(jnp.int32)

    labels = jnp.arange(experts, dtype=jnp.int32)[None, :]
    table = jnp.zeros((rows, experts), jnp.float32)
    for k in range(expert_ids.shape[1]):
        table = table + jnp.where(
            expert_ids[:, k : k + 1] == labels, gate_weights[:, k : k + 1], 0.0
        )
    cold_table = table[:, 1:]
    high = lax.reduce_precision(cold_table, 8, 7)
    rest = cold_table - high
    middle = lax.reduce_precision(rest, 8, 7)
    low = rest - middle
    extra = -(3 * count) % LANES
    payload = jnp.concatenate(
        [
            tokens,
            jnp.pad(
                jnp.concatenate([high, middle, low], axis=1).astype(jnp.bfloat16),
                ((0, 0), (0, extra)),
            ),
        ],
        axis=1,
    )

    def go(block, pairs):
        return lax.ppermute(block, "dp", pairs)

    ahead, behind = {}, {}
    fore = back = payload
    for k in range(1, reach):
        fore, back = go(fore, onward), go(back, backward)
        behind[k], ahead[k] = fore, back
    fore, back = go(fore[: rows // 2], onward), go(back[rows // 2 :], backward)

    hot_blocks = [tokens] + [shifted(tokens, "expert", by) for by in range(1, groups)]
    hot_keep, hot_send = expert_apply(hot_blocks, hot_weights, rows, features, None, 384)

    def serve(blocks):
        others = [go(block, across) for block in blocks]
        kept = sum(block.shape[0] for block in blocks)
        keep, send = expert_apply(blocks + others, cold_weights, kept, features, owner, 256)
        return keep, go(send, across)

    keep, got = serve([payload])
    own = keep + got.astype(jnp.float32)
    sums = {}
    for k in range(1, reach):
        keep, got = serve([ahead[k], behind[k]])
        both = keep + got.astype(jnp.float32)
        sums[k], sums[-k] = both[:rows], both[rows:]
    keep, got = serve([fore, back])
    both = keep + got.astype(jnp.float32)

    half = rows // 2
    fore = go(both[:half].astype(jnp.bfloat16), onward)
    back = go(both[half:].astype(jnp.bfloat16), backward)
    for k in range(reach - 1, 0, -1):
        fore_sum, back_sum = sums[k], sums[-k]
        if k == reach - 1:
            fore = jnp.concatenate([fore_sum[:half] + fore, fore_sum[half:]], axis=0)
            back = jnp.concatenate([back_sum[:half], back_sum[half:] + back], axis=0)
        else:
            fore, back = fore_sum + fore, back_sum + back
        fore, back = go(fore.astype(jnp.bfloat16), onward), go(back.astype(jnp.bfloat16), backward)

    hot = hot_keep
    for by in range(1, groups):
        hot = hot + shifted(hot_send[(by - 1) * rows : by * rows], "expert", -by)
    combined = own + fore.astype(jnp.float32) + back.astype(jnp.float32) + table[:, :1] * hot
    return combined.astype(jnp.bfloat16)


def solution(mesh):
    placed = (
        P(("dp", "expert"), None),
        P(("dp", "expert"), None),
        P(("dp", "expert"), None),
        P(None, None, "expert", None),
        P("dp", None, None, None),
    )
    return jax.shard_map(
        on_device, mesh=mesh, in_specs=placed, out_specs=P(("dp", "expert"), None), check_vma=False
    )
```

```python
import functools

import jax
import jax.numpy as jnp
from jax import lax
from jax.experimental import pallas as pl
from jax.experimental.pallas import tpu as pltpu
from jax.sharding import PartitionSpec as P

LANES = 128
NT = (((1,), (1,)), ((), ()))


def shifted(block, axis, by):
    size = lax.axis_size(axis)
    return lax.ppermute(block, axis, [(i, (i + by) % size) for i in range(size)])


def ring_pairs(count):
    chips = count // 2
    half = chips // 2

    def first_core(place):
        place %= chips
        return 4 * place if place < half else 4 * (chips - 1 - place) + 2

    onward = [
        (first_core(place) + core, first_core(place + 1) + core)
        for place in range(chips)
        for core in range(2)
    ]
    return onward, [(target, source) for source, target in onward]


def expert_kernel(parts, kept_rows, features, scaled, tile, width, owner_ref, *refs):
    blocks, (weight_ref, keep_ref, send_ref, inputs, scale, hidden) = refs[:parts], refs[parts:]
    row = 0
    for block in blocks:
        rows = block.shape[0]
        inputs[row : row + rows, :] = block[:, :features]
        if scaled:
            extra = block[:, features:].astype(jnp.float32)
            lane = lax.broadcasted_iota(jnp.int32, extra.shape, 1)
            owner, count = owner_ref[0], owner_ref[1]
            mine = (lane == owner) | (lane == owner + count) | (lane == owner + 2 * count)
            scale[row : row + rows, :] = jnp.sum(
                jnp.where(mine, extra, 0.0), axis=1, keepdims=True
            )
        row += rows

    units = hidden.shape[1]
    for first in range(0, units, tile):
        some = slice(first, first + tile)
        values = inputs[...]
        gate = lax.dot_general(
            values, weight_ref[0, 0, some, :], NT, preferred_element_type=jnp.float32
        )
        up = lax.dot_general(
            values, weight_ref[0, 1, some, :], NT, preferred_element_type=jnp.float32
        )
        hidden[:, some] = (gate / (1.0 + jnp.exp(-gate)) * up).astype(jnp.bfloat16)
    for first in range(0, features, width):
        some = slice(first, first + width)
        result = jnp.dot(
            hidden[...], weight_ref[0, 2, :, some], preferred_element_type=jnp.float32
        )
        if scaled:
            result = result * scale[...]
        keep_ref[:, some] = result[:kept_rows]
        send_ref[:, some] = result[kept_rows:].astype(jnp.bfloat16)


def expert_apply(blocks, weights, kept_rows, features, owner, tile, width):
    scaled = owner is not None
    if owner is None:
        owner = jnp.zeros((2,), jnp.int32)
    rows = sum(block.shape[0] for block in blocks)
    units = weights.shape[2]
    tile = tile if units % tile == 0 else units
    whole = pl.BlockSpec(memory_space=pltpu.VMEM)
    return pl.pallas_call(
        functools.partial(
            expert_kernel, len(blocks), kept_rows, features, scaled, tile, width
        ),
        in_specs=[pl.BlockSpec(memory_space=pltpu.SMEM)] + [whole] * (len(blocks) + 1),
        out_specs=[whole, whole],
        out_shape=[
            jax.ShapeDtypeStruct((kept_rows, features), jnp.float32),
            jax.ShapeDtypeStruct((rows - kept_rows, features), jnp.bfloat16),
        ],
        scratch_shapes=[
            pltpu.VMEM((rows, features), jnp.bfloat16),
            pltpu.VMEM((rows, 1), jnp.float32),
            pltpu.VMEM((rows, units), jnp.bfloat16),
        ],
        compiler_params=pltpu.CompilerParams(vmem_limit_bytes=32 * 1024 * 1024),
        cost_estimate=pl.CostEstimate(
            flops=6 * rows * units * features,
            bytes_accessed=2 * 3 * units * features + 8 * rows * features,
            transcendentals=rows * units,
        ),
    )(owner, *blocks, weights)


def on_device(tokens, expert_ids, gate_weights, hot_weights, cold_weights):
    rows, features = tokens.shape
    count = lax.axis_size("dp")
    groups = lax.axis_size("expert")
    experts = 1 + count
    onward, backward = ring_pairs(count)
    across = [(i, i ^ 1) for i in range(count)]
    reach = count // 4
    owner = jnp.stack([lax.axis_index("dp"), count]).astype(jnp.int32)

    labels = jnp.arange(experts, dtype=jnp.int32)[None, :]
    table = jnp.zeros((rows, experts), jnp.float32)
    for k in range(expert_ids.shape[1]):
        table = table + jnp.where(
            expert_ids[:, k : k + 1] == labels, gate_weights[:, k : k + 1], 0.0
        )
    cold_table = table[:, 1:]
    high = lax.reduce_precision(cold_table, 8, 7)
    rest = cold_table - high
    middle = lax.reduce_precision(rest, 8, 7)
    low = rest - middle
    extra = -(3 * count) % LANES
    payload = jnp.concatenate(
        [
            tokens,
            jnp.pad(
                jnp.concatenate([high, middle, low], axis=1).astype(jnp.bfloat16),
                ((0, 0), (0, extra)),
            ),
        ],
        axis=1,
    )

    def go(block, pairs):
        return lax.ppermute(block, "dp", pairs)

    def exchange(blocks):
        return [go(block, across) for block in blocks]

    def serve(blocks, others):
        kept = sum(block.shape[0] for block in blocks)
        keep, send = expert_apply(blocks + others, cold_weights, kept, features, owner, 256, 512)
        return keep, send

    def hold(*values):
        return lax.optimization_barrier(values)

    half = rows // 2
    hot_blocks = [tokens] + [shifted(tokens, "expert", by) for by in range(1, groups)]
    fore, back = go(payload, onward), go(payload, backward)
    blocks = [payload]
    others = exchange(blocks)
    served = {}
    for k in range(1, reach + 1):
        result = serve(blocks, others)
        fore, back, *result = hold(fore, back, *result)
        served[k - 1] = result
        blocks = [back, fore]
        others = exchange(blocks)
        if k + 1 < reach:
            fore, back = go(fore, onward), go(back, backward)
        elif k + 1 == reach:
            fore, back = go(fore[:half], onward), go(back[half:], backward)
        else:
            blocks = [fore, back]
            others = exchange(blocks)
            served[reach] = serve(blocks, others)

    hot_keep, hot_send = expert_apply(hot_blocks, hot_weights, rows, features, None, 384, 512)

    def joined(k):
        keep, send = served[k]
        return keep + go(send, across).astype(jnp.float32)

    own = joined(0)
    sums = {}
    for k in range(1, reach):
        both = joined(k)
        sums[k], sums[-k] = both[:rows], both[rows:]
    both = joined(reach)

    fore = go(both[:half].astype(jnp.bfloat16), onward)
    back = go(both[half:].astype(jnp.bfloat16), backward)
    for k in range(reach - 1, 0, -1):
        fore_sum, back_sum = sums[k], sums[-k]
        if k == reach - 1:
            fore = jnp.concatenate([fore_sum[:half] + fore, fore_sum[half:]], axis=0)
            back = jnp.concatenate([back_sum[:half], back_sum[half:] + back], axis=0)
        else:
            fore, back = fore_sum + fore, back_sum + back
        fore, back = go(fore.astype(jnp.bfloat16), onward), go(back.astype(jnp.bfloat16), backward)

    hot = hot_keep
    for by in range(1, groups):
        hot = hot + shifted(hot_send[(by - 1) * rows : by * rows], "expert", -by)
    combined = own + fore.astype(jnp.float32) + back.astype(jnp.float32) + table[:, :1] * hot
    return combined.astype(jnp.bfloat16)


def solution(mesh):
    placed = (
        P(("dp", "expert"), None),
        P(("dp", "expert"), None),
        P(("dp", "expert"), None),
        P(None, None, "expert", None),
        P("dp", None, None, None),
    )
    return jax.shard_map(
        on_device, mesh=mesh, in_specs=placed, out_specs=P(("dp", "expert"), None), check_vma=False
    )
```

```python
import functools

import jax
import jax.numpy as jnp
from jax import lax
from jax.experimental import pallas as pl
from jax.experimental.pallas import tpu as pltpu
from jax.sharding import PartitionSpec as P

LANES = 128
VMEM_BYTES = 12 * 1024 * 1024
NT = (((1,), (1,)), ((), ()))


def shifted(block, axis, by):
    size = lax.axis_size(axis)
    return lax.ppermute(block, axis, [(i, (i + by) % size) for i in range(size)])


def ring_pairs(count):
    chips = count // 2
    half = chips // 2

    def first_core(place):
        place %= chips
        return 4 * place if place < half else 4 * (chips - 1 - place) + 2

    onward = [
        (first_core(place) + core, first_core(place + 1) + core)
        for place in range(chips)
        for core in range(2)
    ]
    return onward, [(target, source) for source, target in onward]


def expert_kernel(parts, experts, features, kept_rows, tile, width, owners_ref, *refs):
    blocks, weights, (keep_ref, *send_ref), (inputs, scales, hidden) = (
        refs[:parts],
        refs[parts : parts + experts],
        refs[parts + experts : -3],
        refs[-3:],
    )
    row = 0
    for block in blocks:
        rows = block.shape[0]
        inputs[row : row + rows, :] = block[:, :features]
        if block.shape[1] > features:
            extra = block[:, features:].astype(jnp.float32)
            lane = lax.broadcasted_iota(jnp.int32, extra.shape, 1)
            count = owners_ref[experts]
            for expert in range(experts):
                owner = owners_ref[expert]
                mine = (lane == owner) | (lane == owner + count) | (lane == owner + 2 * count)
                scales[expert, row : row + rows, :] = jnp.sum(
                    jnp.where(mine, extra, 0.0), axis=1, keepdims=True
                )
        else:
            scales[0, row : row + rows, :] = jnp.ones((rows, 1), jnp.float32)
        row += rows

    units = hidden.shape[2]
    for expert in range(experts):
        for first in range(0, units, tile):
            some = slice(first, first + tile)
            values = inputs[...]
            gate = lax.dot_general(
                values, weights[expert][0, 0, some, :], NT, preferred_element_type=jnp.float32
            )
            up = lax.dot_general(
                values, weights[expert][0, 1, some, :], NT, preferred_element_type=jnp.float32
            )
            hidden[expert, :, some] = (gate / (1.0 + jnp.exp(-gate)) * up).astype(jnp.bfloat16)
    for first in range(0, features, width):
        some = slice(first, first + width)
        result = 0.0
        for expert in range(experts):
            output = jnp.dot(
                hidden[expert], weights[expert][0, 2, :, some], preferred_element_type=jnp.float32
            )
            result = result + output * scales[expert]
        keep_ref[:, some] = result[:kept_rows]
        if send_ref:
            send_ref[0][:, some] = result[kept_rows:].astype(jnp.bfloat16)


def expert_apply(blocks, weights, owners, features, kept_rows, tile=256, width=512):
    rows = sum(block.shape[0] for block in blocks)
    experts = len(weights)
    units = weights[0].shape[2]
    tile = tile if units % tile == 0 else units
    whole = pl.BlockSpec(memory_space=pltpu.VMEM)
    out_shape = [jax.ShapeDtypeStruct((kept_rows, features), jnp.float32)]
    if rows > kept_rows:
        out_shape.append(jax.ShapeDtypeStruct((rows - kept_rows, features), jnp.bfloat16))
    return pl.pallas_call(
        functools.partial(
            expert_kernel, len(blocks), experts, features, kept_rows, tile, width
        ),
        in_specs=[pl.BlockSpec(memory_space=pltpu.SMEM)] + [whole] * (len(blocks) + experts),
        out_specs=[whole] * len(out_shape),
        out_shape=out_shape,
        scratch_shapes=[
            pltpu.VMEM((rows, features), jnp.bfloat16),
            pltpu.VMEM((experts, rows, 1), jnp.float32),
            pltpu.VMEM((experts, rows, units), jnp.bfloat16),
        ],
        compiler_params=pltpu.CompilerParams(vmem_limit_bytes=VMEM_BYTES),
        cost_estimate=pl.CostEstimate(
            flops=6 * rows * units * features * experts,
            bytes_accessed=2 * 3 * units * features * experts + 8 * rows * features,
            transcendentals=rows * units * experts,
        ),
    )(owners, *blocks, *weights)


def stage_kernel(source_ref, target_ref, semaphore):
    copy = pltpu.make_async_copy(source_ref, target_ref, semaphore)
    copy.start()
    copy.wait()


def stage(weights):
    return pl.pallas_call(
        stage_kernel,
        in_specs=[pl.BlockSpec(memory_space=pl.ANY)],
        out_specs=pl.BlockSpec(memory_space=pltpu.VMEM),
        out_shape=jax.ShapeDtypeStruct(weights.shape, weights.dtype),
        scratch_shapes=[pltpu.SemaphoreType.DMA(())],
        compiler_params=pltpu.CompilerParams(vmem_limit_bytes=VMEM_BYTES),
    )(weights)


def on_device(tokens, expert_ids, gate_weights, hot_weights, cold_weights):
    rows, features = tokens.shape
    count = lax.axis_size("dp")
    groups = lax.axis_size("expert")
    experts = 1 + count
    onward, backward = ring_pairs(count)
    across = [(i, i ^ 1) for i in range(count)]
    reach = count // 4
    place = lax.axis_index("dp")
    owners = jnp.stack([place, place ^ 1, count]).astype(jnp.int32)

    labels = jnp.arange(experts, dtype=jnp.int32)[None, :]
    table = jnp.zeros((rows, experts), jnp.float32)
    for k in range(expert_ids.shape[1]):
        table = table + jnp.where(
            expert_ids[:, k : k + 1] == labels, gate_weights[:, k : k + 1], 0.0
        )
    cold_table = table[:, 1:]
    high = lax.reduce_precision(cold_table, 8, 7)
    rest = cold_table - high
    middle = lax.reduce_precision(rest, 8, 7)
    low = rest - middle
    extra = -(3 * count) % LANES
    payload = jnp.concatenate(
        [
            tokens,
            jnp.pad(
                jnp.concatenate([high, middle, low], axis=1).astype(jnp.bfloat16),
                ((0, 0), (0, extra)),
            ),
        ],
        axis=1,
    )

    def go(block, pairs):
        return lax.ppermute(block, "dp", pairs)

    def hold(*values):
        return lax.optimization_barrier(values)

    half = rows // 2
    top, bottom = payload[:half], payload[half:]
    ways = (backward, onward)

    def move(blocks):
        return [go(block, way) for block, way in zip(blocks, ways)]

    short = move([top, bottom])
    long = move([bottom, top])
    mine, other = hold(stage(cold_weights), go(cold_weights, across))
    pair = [mine, stage(other)]

    def serve(blocks):
        kept = sum(block.shape[0] for block in blocks)
        return expert_apply(blocks, pair, owners, features, kept)[0]

    sums = {}
    for k in range(1, reach - 1):
        here, there = short, long
        short, long = move(short), move(long)
        both = serve(here + there)
        *short, both = hold(*short, both)
        sums["short", k], sums["long", k] = both[:rows], both[rows:]
    last = reach - 1
    both = serve(short)
    *long, both = hold(*long, both)
    sums["short", last] = both
    here, long = long, move(long)
    both = serve(here)
    *long, both = hold(*long, both)
    sums["long", last] = both
    sums["long", reach] = serve(long)

    def move_on(values):
        return [go(value.astype(jnp.bfloat16), way) for value, way in zip(values, (onward, backward))]

    def grow(moving, mine):
        return move_on([mine[:half] + moving[0], mine[half:] + moving[1]])

    short = move_on([sums["short", last][:half], sums["short", last][half:]])
    long = move_on([sums["long", reach][:half], sums["long", reach][half:]])
    for k in range(last, 0, -1):
        if k > 1:
            short = grow(short, sums["short", k - 1])
        long = grow(long, sums["long", k])

    worked, own_block, own_tokens = hold(sums["long", reach], payload, tokens)
    hot_blocks = [own_tokens] + [shifted(own_tokens, "expert", by) for by in range(1, groups)]
    hot, hot_send = expert_apply(
        hot_blocks, [hot_weights], owners[1:], features, rows, tile=384
    )
    for by in range(1, groups):
        hot = hot + shifted(hot_send[(by - 1) * rows : by * rows], "expert", -by)
    (base,) = hold(serve([own_block]) + table[:, :1] * hot)
    combined = [
        base[:half] + short[0].astype(jnp.float32) + long[1].astype(jnp.float32),
        base[half:] + short[1].astype(jnp.float32) + long[0].astype(jnp.float32),
    ]
    return jnp.concatenate(combined, axis=0).astype(jnp.bfloat16)


def solution(mesh):
    placed = (
        P(("dp", "expert"), None),
        P(("dp", "expert"), None),
        P(("dp", "expert"), None),
        P(None, None, "expert", None),
        P("dp", None, None, None),
    )
    return jax.shard_map(
        on_device, mesh=mesh, in_specs=placed, out_specs=P(("dp", "expert"), None), check_vma=False
    )
```

```python
import functools

import jax
import jax.numpy as jnp
from jax import lax
from jax.experimental import pallas as pl
from jax.experimental.pallas import tpu as pltpu
from jax.sharding import PartitionSpec as P

LANES = 128
VMEM_BYTES = 12 * 1024 * 1024
NT = (((1,), (1,)), ((), ()))


def shifted(block, axis, by):
    size = lax.axis_size(axis)
    return lax.ppermute(block, axis, [(i, (i + by) % size) for i in range(size)])


def ring_pairs(count):
    chips = count // 2
    half = chips // 2

    def first_core(place):
        place %= chips
        return 4 * place if place < half else 4 * (chips - 1 - place) + 2

    onward = [
        (first_core(place) + core, first_core(place + 1) + core)
        for place in range(chips)
        for core in range(2)
    ]
    return onward, [(target, source) for source, target in onward]


def expert_kernel(parts, experts, features, kept_rows, tile, width, marks, owners_ref, *refs):
    refs = refs[marks:]
    blocks, weights, (keep_ref, *send_ref), (inputs, scales, hidden) = (
        refs[:parts],
        refs[parts : parts + experts],
        refs[parts + experts : -3],
        refs[-3:],
    )
    row = 0
    for block in blocks:
        rows = block.shape[0]
        inputs[row : row + rows, :] = block[:, :features]
        if block.shape[1] > features:
            extra = block[:, features:].astype(jnp.float32)
            lane = lax.broadcasted_iota(jnp.int32, extra.shape, 1)
            count = owners_ref[experts]
            for expert in range(experts):
                owner = owners_ref[expert]
                mine = (lane == owner) | (lane == owner + count) | (lane == owner + 2 * count)
                scales[expert, row : row + rows, :] = jnp.sum(
                    jnp.where(mine, extra, 0.0), axis=1, keepdims=True
                )
        else:
            scales[0, row : row + rows, :] = jnp.ones((rows, 1), jnp.float32)
        row += rows

    units = hidden.shape[2]
    for expert in range(experts):
        for first in range(0, units, tile):
            some = slice(first, first + tile)
            values = inputs[...]
            gate = lax.dot_general(
                values, weights[expert][0, 0, some, :], NT, preferred_element_type=jnp.float32
            )
            up = lax.dot_general(
                values, weights[expert][0, 1, some, :], NT, preferred_element_type=jnp.float32
            )
            hidden[expert, :, some] = (gate / (1.0 + jnp.exp(-gate)) * up).astype(jnp.bfloat16)
    for first in range(0, features, width):
        some = slice(first, first + width)
        result = 0.0
        for expert in range(experts):
            output = jnp.dot(
                hidden[expert], weights[expert][0, 2, :, some], preferred_element_type=jnp.float32
            )
            result = result + output * scales[expert]
        keep_ref[:, some] = result[:kept_rows]
        if send_ref:
            send_ref[0][:, some] = result[kept_rows:].astype(jnp.bfloat16)


def expert_apply(blocks, weights, owners, features, kept_rows, tile=256, width=512, after=None):
    marks = [] if after is None else [after]
    rows = sum(block.shape[0] for block in blocks)
    experts = len(weights)
    units = weights[0].shape[2]
    tile = tile if units % tile == 0 else units
    whole = pl.BlockSpec(memory_space=pltpu.VMEM)
    out_shape = [jax.ShapeDtypeStruct((kept_rows, features), jnp.float32)]
    if rows > kept_rows:
        out_shape.append(jax.ShapeDtypeStruct((rows - kept_rows, features), jnp.bfloat16))
    return pl.pallas_call(
        functools.partial(
            expert_kernel, len(blocks), experts, features, kept_rows, tile, width, len(marks)
        ),
        in_specs=[pl.BlockSpec(memory_space=pltpu.SMEM)]
        + [pl.BlockSpec(memory_space=pl.ANY)] * len(marks)
        + [whole] * (len(blocks) + experts),
        out_specs=[whole] * len(out_shape),
        out_shape=out_shape,
        scratch_shapes=[
            pltpu.VMEM((rows, features), jnp.bfloat16),
            pltpu.VMEM((experts, rows, 1), jnp.float32),
            pltpu.VMEM((experts, rows, units), jnp.bfloat16),
        ],
        compiler_params=pltpu.CompilerParams(vmem_limit_bytes=VMEM_BYTES),
        cost_estimate=pl.CostEstimate(
            flops=6 * rows * units * features * experts,
            bytes_accessed=2 * 3 * units * features * experts + 8 * rows * features,
            transcendentals=rows * units * experts,
        ),
    )(owners, *marks, *blocks, *weights)


def stage_kernel(source_ref, other_ref, target_ref, mark_ref, semaphore):
    copy = pltpu.make_async_copy(source_ref, target_ref, semaphore)
    copy.start()
    mark_ref[...] = jnp.zeros(mark_ref.shape, jnp.float32)
    copy.wait()


def stage(weights, beside):
    return pl.pallas_call(
        stage_kernel,
        in_specs=[pl.BlockSpec(memory_space=pl.ANY)] * 2,
        out_specs=[pl.BlockSpec(memory_space=pltpu.VMEM)] * 2,
        out_shape=[
            jax.ShapeDtypeStruct(weights.shape, weights.dtype),
            jax.ShapeDtypeStruct((8, LANES), jnp.float32),
        ],
        scratch_shapes=[pltpu.SemaphoreType.DMA(())],
        compiler_params=pltpu.CompilerParams(vmem_limit_bytes=VMEM_BYTES),
    )(weights, beside)


def payload_kernel(count, tokens_ref, ids_ref, gates_ref, top_ref, bottom_ref, hot_ref):
    rows, features = tokens_ref.shape
    half = rows // 2
    top_ref[:, :features] = tokens_ref[:half, :]
    bottom_ref[:, :features] = tokens_ref[half:, :]
    ids, gates = ids_ref[...], gates_ref[...]
    line = lax.broadcasted_iota(jnp.int32, (top_ref.shape[1] - features, rows), 0)
    part = (line >= count).astype(jnp.int32) + (line >= 2 * count).astype(jnp.int32)
    label = line - part * count + 1
    table = jnp.zeros(line.shape, jnp.float32)
    for k in range(ids.shape[0]):
        table = table + jnp.where(ids[k : k + 1, :] == label, gates[k : k + 1, :], 0.0)
    high = table.astype(jnp.bfloat16).astype(jnp.float32)
    rest = table - high
    middle = rest.astype(jnp.bfloat16).astype(jnp.float32)
    value = jnp.where(part == 0, high, jnp.where(part == 1, middle, rest - middle))
    value = jnp.where(line < 3 * count, value, 0.0).T.astype(jnp.bfloat16)
    top_ref[:, features:] = value[:half]
    bottom_ref[:, features:] = value[half:]
    hot = jnp.sum(jnp.where(ids == 0, gates, 0.0), axis=0, keepdims=True)
    hot_ref[...] = jnp.broadcast_to(hot, (LANES, rows)).T[:, :1]


def make_payload(tokens, expert_ids, gate_weights, count):
    rows, features = tokens.shape
    width = features + 3 * count + -(3 * count) % LANES
    whole = pl.BlockSpec(memory_space=pltpu.VMEM)
    block = jax.ShapeDtypeStruct((rows // 2, width), tokens.dtype)
    return pl.pallas_call(
        functools.partial(payload_kernel, count),
        in_specs=[whole] * 3,
        out_specs=[whole] * 3,
        out_shape=[block, block, jax.ShapeDtypeStruct((rows, 1), jnp.float32)],
        compiler_params=pltpu.CompilerParams(vmem_limit_bytes=VMEM_BYTES),
    )(tokens, expert_ids.T, gate_weights.T)


def on_device(tokens, expert_ids, gate_weights, hot_weights, cold_weights):
    rows, features = tokens.shape
    count = lax.axis_size("dp")
    groups = lax.axis_size("expert")
    onward, backward = ring_pairs(count)
    across = [(i, i ^ 1) for i in range(count)]
    reach = count // 4
    last = reach - 1
    half = rows // 2
    place = lax.axis_index("dp")
    owners = jnp.stack([place, place ^ 1, count]).astype(jnp.int32)

    def go(block, pairs):
        return lax.ppermute(block, "dp", pairs)

    def move(blocks):
        return [go(block, way) for block, way in zip(blocks, (backward, onward))]

    def hold(*values):
        return lax.optimization_barrier(values)

    top, bottom, hot_gate = make_payload(tokens, expert_ids, gate_weights, count)
    short = move([top, bottom])
    long = move([bottom, top])
    other, staged = stage(go(cold_weights, across), cold_weights)
    pair = [cold_weights, other]
    *both, staged = hold(*short, *long, staged)
    short, long = both[:2], both[2:]

    def serve(blocks):
        kept = sum(block.shape[0] for block in blocks)
        return expert_apply(blocks, pair, owners, features, kept, after=staged)[0]

    sums = {}
    for k in range(1, reach):
        here = short + long
        if k < last:
            short = move(short)
        long = move(long)
        both = serve(here)
        *long, both = hold(*long, both)
        sums["short", k], sums["long", k] = both[:rows], both[rows:]
    both = serve(long + [top, bottom])
    sums["long", reach], sums["own"] = both[:rows], both[rows:]

    def move_on(values):
        return [go(value.astype(jnp.bfloat16), way) for value, way in zip(values, (onward, backward))]

    def grow(moving, mine):
        return move_on([mine[:half] + moving[0], mine[half:] + moving[1]])

    short = move_on([sums["short", last][:half], sums["short", last][half:]])
    long = move_on([sums["long", reach][:half], sums["long", reach][half:]])
    for k in range(last, 0, -1):
        if k > 1:
            short = grow(short, sums["short", k - 1])
        long = grow(long, sums["long", k])

    hot_blocks = [tokens] + [shifted(tokens, "expert", by) for by in range(1, groups)]
    hot, hot_send = expert_apply(
        hot_blocks, [hot_weights], owners[1:], features, rows, tile=384
    )
    for by in range(1, groups):
        hot = hot + shifted(hot_send[(by - 1) * rows : by * rows], "expert", -by)
    (base,) = hold(sums["own"] + hot_gate * hot)
    combined = [
        base[:half] + short[0].astype(jnp.float32) + long[1].astype(jnp.float32),
        base[half:] + short[1].astype(jnp.float32) + long[0].astype(jnp.float32),
    ]
    return jnp.concatenate(combined, axis=0).astype(jnp.bfloat16)


def solution(mesh):
    placed = (
        P(("dp", "expert"), None),
        P(("dp", "expert"), None),
        P(("dp", "expert"), None),
        P(None, None, "expert", None),
        P("dp", None, None, None),
    )
    return jax.shard_map(
        on_device, mesh=mesh, in_specs=placed, out_specs=P(("dp", "expert"), None), check_vma=False
    )
```

```python
import functools

import jax
import jax.numpy as jnp
from jax import lax
from jax.experimental import pallas as pl
from jax.experimental.pallas import tpu as pltpu
from jax.sharding import PartitionSpec as P

LANES = 128
VMEM_BYTES = 12 * 1024 * 1024
NT = (((1,), (1,)), ((), ()))


def shifted(block, axis, by):
    size = lax.axis_size(axis)
    return lax.ppermute(block, axis, [(i, (i + by) % size) for i in range(size)])


def ring_pairs(count):
    chips = count // 2
    half = chips // 2

    def first_core(place):
        place %= chips
        return 4 * place if place < half else 4 * (chips - 1 - place) + 2

    onward = [
        (first_core(place) + core, first_core(place + 1) + core)
        for place in range(chips)
        for core in range(2)
    ]
    return onward, [(target, source) for source, target in onward]


def expert_kernel(parts, experts, features, tile, width, marks, owners_ref, *refs):
    refs = refs[marks:]
    blocks, weights, outs, (inputs, scales, hidden) = (
        refs[:parts],
        refs[parts : parts + experts],
        refs[parts + experts : -3],
        refs[-3:],
    )
    row = 0
    for block in blocks:
        rows = block.shape[0]
        inputs[row : row + rows, :] = block[:, :features]
        if block.shape[1] > features:
            extra = block[:, features:].astype(jnp.float32)
            lane = lax.broadcasted_iota(jnp.int32, extra.shape, 1)
            count = owners_ref[experts]
            for expert in range(experts):
                owner = owners_ref[expert]
                mine = (lane == owner) | (lane == owner + count) | (lane == owner + 2 * count)
                scales[expert, row : row + rows, :] = jnp.sum(
                    jnp.where(mine, extra, 0.0), axis=1, keepdims=True
                )
        else:
            scales[0, row : row + rows, :] = jnp.ones((rows, 1), jnp.float32)
        row += rows

    units = hidden.shape[2]
    for expert in range(experts):
        for first in range(0, units, tile):
            some = slice(first, first + tile)
            values = inputs[...]
            gate = lax.dot_general(
                values, weights[expert][0, 0, some, :], NT, preferred_element_type=jnp.float32
            )
            up = lax.dot_general(
                values, weights[expert][0, 1, some, :], NT, preferred_element_type=jnp.float32
            )
            hidden[expert, :, some] = (gate / (1.0 + jnp.exp(-gate)) * up).astype(jnp.bfloat16)
    for first in range(0, features, width):
        some = slice(first, first + width)
        result = 0.0
        for expert in range(experts):
            output = jnp.dot(
                hidden[expert], weights[expert][0, 2, :, some], preferred_element_type=jnp.float32
            )
            result = result + output * scales[expert]
        row = 0
        for out in outs:
            rows = out.shape[0]
            out[:, some] = result[row : row + rows].astype(out.dtype)
            row += rows


def expert_apply(blocks, weights, owners, features, kept_rows, tile=256, width=512, after=None):
    marks = [] if after is None else [after]
    rows = sum(block.shape[0] for block in blocks)
    experts = len(weights)
    units = weights[0].shape[2]
    tile = tile if units % tile == 0 else units
    whole = pl.BlockSpec(memory_space=pltpu.VMEM)
    out_shape, row = [], 0
    for block in blocks:
        out_type = jnp.float32 if row < kept_rows else jnp.bfloat16
        out_shape.append(jax.ShapeDtypeStruct((block.shape[0], features), out_type))
        row += block.shape[0]
    return pl.pallas_call(
        functools.partial(
            expert_kernel, len(blocks), experts, features, tile, width, len(marks)
        ),
        in_specs=[pl.BlockSpec(memory_space=pltpu.SMEM)]
        + [pl.BlockSpec(memory_space=pl.ANY)] * len(marks)
        + [whole] * (len(blocks) + experts),
        out_specs=[whole] * len(out_shape),
        out_shape=out_shape,
        scratch_shapes=[
            pltpu.VMEM((rows, features), jnp.bfloat16),
            pltpu.VMEM((experts, rows, 1), jnp.float32),
            pltpu.VMEM((experts, rows, units), jnp.bfloat16),
        ],
        compiler_params=pltpu.CompilerParams(vmem_limit_bytes=VMEM_BYTES),
        cost_estimate=pl.CostEstimate(
            flops=6 * rows * units * features * experts,
            bytes_accessed=2 * 3 * units * features * experts + 8 * rows * features,
            transcendentals=rows * units * experts,
        ),
    )(owners, *marks, *blocks, *weights)


def stage_kernel(source_ref, other_ref, target_ref, mark_ref, semaphore):
    copy = pltpu.make_async_copy(source_ref, target_ref, semaphore)
    copy.start()
    mark_ref[...] = jnp.zeros(mark_ref.shape, jnp.float32)
    copy.wait()


def stage(weights, beside):
    return pl.pallas_call(
        stage_kernel,
        in_specs=[pl.BlockSpec(memory_space=pl.ANY)] * 2,
        out_specs=[pl.BlockSpec(memory_space=pltpu.VMEM)] * 2,
        out_shape=[
            jax.ShapeDtypeStruct(weights.shape, weights.dtype),
            jax.ShapeDtypeStruct((8, LANES), jnp.float32),
        ],
        scratch_shapes=[pltpu.SemaphoreType.DMA(())],
        compiler_params=pltpu.CompilerParams(vmem_limit_bytes=VMEM_BYTES),
    )(weights, beside)


def payload_kernel(count, tokens_ref, ids_ref, gates_ref, top_ref, bottom_ref, hot_ref):
    rows, features = tokens_ref.shape
    half = rows // 2
    top_ref[:, :features] = tokens_ref[:half, :]
    bottom_ref[:, :features] = tokens_ref[half:, :]
    ids, gates = ids_ref[...], gates_ref[...]
    line = lax.broadcasted_iota(jnp.int32, (top_ref.shape[1] - features, rows), 0)
    part = (line >= count).astype(jnp.int32) + (line >= 2 * count).astype(jnp.int32)
    label = line - part * count + 1
    table = jnp.zeros(line.shape, jnp.float32)
    for k in range(ids.shape[0]):
        table = table + jnp.where(ids[k : k + 1, :] == label, gates[k : k + 1, :], 0.0)
    high = table.astype(jnp.bfloat16).astype(jnp.float32)
    rest = table - high
    middle = rest.astype(jnp.bfloat16).astype(jnp.float32)
    value = jnp.where(part == 0, high, jnp.where(part == 1, middle, rest - middle))
    value = jnp.where(line < 3 * count, value, 0.0).T.astype(jnp.bfloat16)
    top_ref[:, features:] = value[:half]
    bottom_ref[:, features:] = value[half:]
    hot = jnp.sum(jnp.where(ids == 0, gates, 0.0), axis=0, keepdims=True)
    hot_ref[...] = jnp.broadcast_to(hot, (LANES, rows)).T[:, :1]


def make_payload(tokens, expert_ids, gate_weights, count):
    rows, features = tokens.shape
    width = features + 3 * count + -(3 * count) % LANES
    whole = pl.BlockSpec(memory_space=pltpu.VMEM)
    block = jax.ShapeDtypeStruct((rows // 2, width), tokens.dtype)
    return pl.pallas_call(
        functools.partial(payload_kernel, count),
        in_specs=[whole] * 3,
        out_specs=[whole] * 3,
        out_shape=[block, block, jax.ShapeDtypeStruct((rows, 1), jnp.float32)],
        compiler_params=pltpu.CompilerParams(vmem_limit_bytes=VMEM_BYTES),
    )(tokens, expert_ids.T, gate_weights.T)


def on_device(tokens, expert_ids, gate_weights, hot_weights, cold_weights):
    rows, features = tokens.shape
    count = lax.axis_size("dp")
    groups = lax.axis_size("expert")
    onward, backward = ring_pairs(count)
    across = [(i, i ^ 1) for i in range(count)]
    reach = count // 4
    last = reach - 1
    half = rows // 2
    place = lax.axis_index("dp")
    owners = jnp.stack([place, place ^ 1, count]).astype(jnp.int32)

    def go(block, pairs):
        return lax.ppermute(block, "dp", pairs)

    def move(blocks):
        return [go(block, way) for block, way in zip(blocks, (backward, onward))]

    def hold(*values):
        return lax.optimization_barrier(values)

    top, bottom, hot_gate = make_payload(tokens, expert_ids, gate_weights, count)
    short = move([top, bottom])
    long = move([bottom, top])
    other, staged = stage(go(cold_weights, across), cold_weights)
    pair = [cold_weights, other]
    *both, staged, own_tokens = hold(*short, *long, staged, tokens)
    short, long = both[:2], both[2:]

    def serve(blocks):
        kept = sum(block.shape[0] for block in blocks)
        return expert_apply(blocks, pair, owners, features, kept, after=staged)

    sums = {}
    for k in range(1, reach):
        here = short + long
        if k < last:
            short = move(short)
        long = move(long)
        *long, first, second, third, fourth = hold(*long, *serve(here))
        sums["short", k], sums["long", k] = [first, second], [third, fourth]
    *sums["long", reach], own_top, own_bottom = serve(long + [top, bottom])

    def move_on(values):
        return [go(value.astype(jnp.bfloat16), way) for value, way in zip(values, (onward, backward))]

    def grow(moving, mine):
        return move_on([mine[0] + moving[0], mine[1] + moving[1]])

    short = move_on(sums["short", last])
    *short, first, second = hold(*short, *sums["long", reach])
    long = move_on([first, second])
    for k in range(last, 0, -1):
        if k > 1:
            short = grow(short, sums["short", k - 1])
        long = grow(long, sums["long", k])

    hot_blocks = [own_tokens] + [shifted(own_tokens, "expert", by) for by in range(1, groups)]
    hot, *hot_send = expert_apply(
        hot_blocks, [hot_weights], owners[1:], features, rows, tile=384
    )
    for by in range(1, groups):
        hot = hot + shifted(hot_send[by - 1], "expert", -by)
    hot = hot_gate * hot
    own_top, own_bottom = hold(own_top + hot[:half], own_bottom + hot[half:])
    combined = [
        own_top + short[0].astype(jnp.float32) + long[1].astype(jnp.float32),
        own_bottom + short[1].astype(jnp.float32) + long[0].astype(jnp.float32),
    ]
    return jnp.concatenate(combined, axis=0).astype(jnp.bfloat16)


def solution(mesh):
    placed = (
        P(("dp", "expert"), None),
        P(("dp", "expert"), None),
        P(("dp", "expert"), None),
        P(None, None, "expert", None),
        P("dp", None, None, None),
    )
    return jax.shard_map(
        on_device, mesh=mesh, in_specs=placed, out_specs=P(("dp", "expert"), None), check_vma=False
    )
```

```python
import functools

import jax
import jax.numpy as jnp
from jax import lax
from jax.experimental import pallas as pl
from jax.experimental.pallas import tpu as pltpu
from jax.sharding import PartitionSpec as P

LANES = 128
VMEM_BYTES = 12 * 1024 * 1024
NT = (((1,), (1,)), ((), ()))


def shifted(block, axis, by):
    size = lax.axis_size(axis)
    return lax.ppermute(block, axis, [(i, (i + by) % size) for i in range(size)])


def ring_pairs(count):
    chips = count // 2
    half = chips // 2

    def first_core(place):
        place %= chips
        return 4 * place if place < half else 4 * (chips - 1 - place) + 2

    onward = [
        (first_core(place) + core, first_core(place + 1) + core)
        for place in range(chips)
        for core in range(2)
    ]
    return onward, [(target, source) for source, target in onward]


def expert_kernel(parts, experts, features, tile, width, marks, owners_ref, *refs):
    refs = refs[marks:]
    blocks, weights, outs, (inputs, scales, hidden) = (
        refs[:parts],
        refs[parts : parts + experts],
        refs[parts + experts : -3],
        refs[-3:],
    )
    row = 0
    for block in blocks:
        rows = block.shape[0]
        inputs[row : row + rows, :] = block[:, :features]
        if block.shape[1] > features:
            extra = block[:, features:].astype(jnp.float32)
            lane = lax.broadcasted_iota(jnp.int32, extra.shape, 1)
            count = owners_ref[experts]
            for expert in range(experts):
                owner = owners_ref[expert]
                mine = (lane == owner) | (lane == owner + count) | (lane == owner + 2 * count)
                scales[expert, row : row + rows, :] = jnp.sum(
                    jnp.where(mine, extra, 0.0), axis=1, keepdims=True
                )
        else:
            scales[0, row : row + rows, :] = jnp.ones((rows, 1), jnp.float32)
        row += rows

    units = hidden.shape[2]
    for expert in range(experts):
        for first in range(0, units, tile):
            some = slice(first, first + tile)
            values = inputs[...]
            gate = lax.dot_general(
                values, weights[expert][0, 0, some, :], NT, preferred_element_type=jnp.float32
            )
            up = lax.dot_general(
                values, weights[expert][0, 1, some, :], NT, preferred_element_type=jnp.float32
            )
            hidden[expert, :, some] = (gate / (1.0 + jnp.exp(-gate)) * up).astype(jnp.bfloat16)
    for first in range(0, features, width):
        some = slice(first, first + width)
        result = 0.0
        for expert in range(experts):
            output = jnp.dot(
                hidden[expert], weights[expert][0, 2, :, some], preferred_element_type=jnp.float32
            )
            result = result + output * scales[expert]
        row = 0
        for out in outs:
            rows = out.shape[0]
            out[:, some] = result[row : row + rows].astype(out.dtype)
            row += rows


def expert_apply(blocks, weights, owners, features, kept_rows, tile=256, width=512, after=None):
    marks = [] if after is None else [after]
    rows = sum(block.shape[0] for block in blocks)
    experts = len(weights)
    units = weights[0].shape[2]
    tile = tile if units % tile == 0 else units
    whole = pl.BlockSpec(memory_space=pltpu.VMEM)
    out_shape, row = [], 0
    for block in blocks:
        out_type = jnp.float32 if row < kept_rows else jnp.bfloat16
        out_shape.append(jax.ShapeDtypeStruct((block.shape[0], features), out_type))
        row += block.shape[0]
    return pl.pallas_call(
        functools.partial(
            expert_kernel, len(blocks), experts, features, tile, width, len(marks)
        ),
        in_specs=[pl.BlockSpec(memory_space=pltpu.SMEM)]
        + [pl.BlockSpec(memory_space=pl.ANY)] * len(marks)
        + [whole] * (len(blocks) + experts),
        out_specs=[whole] * len(out_shape),
        out_shape=out_shape,
        scratch_shapes=[
            pltpu.VMEM((rows, features), jnp.bfloat16),
            pltpu.VMEM((experts, rows, 1), jnp.float32),
            pltpu.VMEM((experts, rows, units), jnp.bfloat16),
        ],
        compiler_params=pltpu.CompilerParams(vmem_limit_bytes=VMEM_BYTES),
        cost_estimate=pl.CostEstimate(
            flops=6 * rows * units * features * experts,
            bytes_accessed=2 * 3 * units * features * experts + 8 * rows * features,
            transcendentals=rows * units * experts,
        ),
    )(owners, *marks, *blocks, *weights)


def stage_kernel(source_ref, other_ref, target_ref, mark_ref, semaphore):
    copy = pltpu.make_async_copy(source_ref, target_ref, semaphore)
    copy.start()
    mark_ref[...] = jnp.zeros(mark_ref.shape, jnp.float32)
    copy.wait()


def stage(weights, beside):
    return pl.pallas_call(
        stage_kernel,
        in_specs=[pl.BlockSpec(memory_space=pl.ANY)] * 2,
        out_specs=[pl.BlockSpec(memory_space=pltpu.VMEM)] * 2,
        out_shape=[
            jax.ShapeDtypeStruct(weights.shape, weights.dtype),
            jax.ShapeDtypeStruct((8, LANES), jnp.float32),
        ],
        scratch_shapes=[pltpu.SemaphoreType.DMA(())],
        compiler_params=pltpu.CompilerParams(vmem_limit_bytes=VMEM_BYTES),
    )(weights, beside)


def payload_kernel(count, tokens_ref, ids_ref, gates_ref, top_ref, bottom_ref, hot_ref):
    rows, features = tokens_ref.shape
    half = rows // 2
    top_ref[:, :features] = tokens_ref[:half, :]
    bottom_ref[:, :features] = tokens_ref[half:, :]
    ids, gates = ids_ref[...], gates_ref[...]
    line = lax.broadcasted_iota(jnp.int32, (top_ref.shape[1] - features, rows), 0)
    part = (line >= count).astype(jnp.int32) + (line >= 2 * count).astype(jnp.int32)
    label = line - part * count + 1
    table = jnp.zeros(line.shape, jnp.float32)
    for k in range(ids.shape[0]):
        table = table + jnp.where(ids[k : k + 1, :] == label, gates[k : k + 1, :], 0.0)
    high = table.astype(jnp.bfloat16).astype(jnp.float32)
    rest = table - high
    middle = rest.astype(jnp.bfloat16).astype(jnp.float32)
    value = jnp.where(part == 0, high, jnp.where(part == 1, middle, rest - middle))
    value = jnp.where(line < 3 * count, value, 0.0).T.astype(jnp.bfloat16)
    top_ref[:, features:] = value[:half]
    bottom_ref[:, features:] = value[half:]
    hot = jnp.sum(jnp.where(ids == 0, gates, 0.0), axis=0, keepdims=True)
    hot_ref[...] = jnp.broadcast_to(hot, (LANES, rows)).T[:, :1]


def make_payload(tokens, expert_ids, gate_weights, count):
    rows, features = tokens.shape
    width = features + 3 * count + -(3 * count) % LANES
    whole = pl.BlockSpec(memory_space=pltpu.VMEM)
    block = jax.ShapeDtypeStruct((rows // 2, width), tokens.dtype)
    return pl.pallas_call(
        functools.partial(payload_kernel, count),
        in_specs=[whole] * 3,
        out_specs=[whole] * 3,
        out_shape=[block, block, jax.ShapeDtypeStruct((rows, 1), jnp.float32)],
        compiler_params=pltpu.CompilerParams(vmem_limit_bytes=VMEM_BYTES),
    )(tokens, expert_ids.T, gate_weights.T)


def on_device(tokens, expert_ids, gate_weights, hot_weights, cold_weights):
    rows, features = tokens.shape
    count = lax.axis_size("dp")
    groups = lax.axis_size("expert")
    onward, backward = ring_pairs(count)
    across = [(i, i ^ 1) for i in range(count)]
    reach = count // 4
    last = reach - 1
    half = rows // 2
    place = lax.axis_index("dp")
    owners = jnp.stack([place, place ^ 1, count]).astype(jnp.int32)

    def go(block, pairs):
        return lax.ppermute(block, "dp", pairs)

    def move(blocks):
        return [go(block, way) for block, way in zip(blocks, (backward, onward))]

    def hold(*values):
        return lax.optimization_barrier(values)

    top, bottom, hot_gate = make_payload(tokens, expert_ids, gate_weights, count)
    short = move([top, bottom])
    long = move([bottom, top])
    other, staged = stage(go(cold_weights, across), cold_weights)
    pair = [cold_weights, other]
    *both, staged = hold(*short, *long, staged)
    short, long = both[:2], both[2:]

    def serve(blocks):
        kept = sum(block.shape[0] for block in blocks)
        return expert_apply(blocks, pair, owners, features, kept, after=staged)

    sums = {}
    for k in range(1, reach):
        here = short + long
        if k < last:
            short = move(short)
        long = move(long)
        *long, first, second, third, fourth = hold(*long, *serve(here))
        sums["short", k], sums["long", k] = [first, second], [third, fourth]
    *sums["long", reach], own_top, own_bottom = serve(long + [top, bottom])

    def move_on(values):
        return [go(value.astype(jnp.bfloat16), way) for value, way in zip(values, (onward, backward))]

    def grow(moving, mine):
        return move_on([mine[0] + moving[0], mine[1] + moving[1]])

    short = move_on(sums["short", last])
    *short, first, second, own_tokens = hold(*short, *sums["long", reach], tokens)
    long = move_on([first, second])
    for k in range(last, 0, -1):
        if k > 1:
            short = grow(short, sums["short", k - 1])
        long = grow(long, sums["long", k])

    hot_blocks = [own_tokens] + [shifted(own_tokens, "expert", by) for by in range(1, groups)]
    hot, *hot_send = expert_apply(
        hot_blocks, [hot_weights], owners[1:], features, rows, tile=384
    )
    for by in range(1, groups):
        hot = hot + shifted(hot_send[by - 1], "expert", -by)
    hot = hot_gate * hot
    own_top, own_bottom = hold(own_top + hot[:half], own_bottom + hot[half:])
    combined = [
        own_top + short[0].astype(jnp.float32) + long[1].astype(jnp.float32),
        own_bottom + short[1].astype(jnp.float32) + long[0].astype(jnp.float32),
    ]
    return jnp.concatenate(combined, axis=0).astype(jnp.bfloat16)


def solution(mesh):
    placed = (
        P(("dp", "expert"), None),
        P(("dp", "expert"), None),
        P(("dp", "expert"), None),
        P(None, None, "expert", None),
        P("dp", None, None, None),
    )
    return jax.shard_map(
        on_device, mesh=mesh, in_specs=placed, out_specs=P(("dp", "expert"), None), check_vma=False
    )
```
